256 devices in a mesh: grp: 8 (over y, core), seq: 32 (over z, x).
Axes of the slice: x: 4, y: 4, z: 8, core: 2. Of those that a mesh axis runs over, the one named last changes fastest.
Arguments:
- queries: bfloat16 [32768, 8192], P(('grp', 'seq')), may hold values from -120 to 120
- key_rows: bfloat16 [32768, 512], P(('grp', 'seq')), may hold values from -6 to 6
- value_rows: bfloat16 [32768, 512], P(('grp', 'seq')), may hold values from -6 to 6
- grad_rows: bfloat16 [32768, 8192], P(('grp', 'seq')), may hold values from -6 to 6
- targets: int32 [32768], P(('grp', 'seq')), may hold values from 0 to 32767, as said below
- doc_lengths: int32 [8, 16], P('grp'), may hold values from 1 to 512, 4096 in all within a row
Outputs:
- grad_query: bfloat16 [32768, 8192], P(('grp', 'seq'))
- grad_key: bfloat16 [32768, 512], P(('grp', 'seq'))
- grad_value: bfloat16 [32768, 512], P(('grp', 'seq'))
The draws below stay inside these ranges and needn't reach their ends.
Inputs may be any that keep to these rules, and one draw needn't show every extreme that they name: targets is a permutation of the 32768 grouped rows; the grouped row of a loader row lies on the device with the same seq index in the group given by the row; at most 24 rows of one device go to one device, and every device receives exactly 24 rows from some device.
All inputs are finite; a program needn't handle non-finite values.
Results may differ from the reference program's by a relative error of at most 0.0095.
Values may be sent and summed in bfloat16 or wider, within the bound.
No kernel may reach another device: no remote copies, remote signals or barrier semaphores. Data moves between devices by JAX's collectives and lax.ppermute only.
A program may use at most 64 MiB of HBM per device.

```python
import math
import jax
import jax.numpy as jnp
import numpy as np
from jax import lax

HQ = 64
KVH = 4
HD = 128
TOK_DEV = 128
MAXDOC = 512
TILE = 256
GQ = 16
GROUP_LEN = 4096
TOKENS = 32768
CAP = 24
DOCS = 16
N_GRP = 8
N_SEQ = 32


def shared_keys(key):
    return jnp.clip(jax.random.normal(key, (TOKENS, KVH * HD), jnp.float32), -6.0, 6.0)


def draw_key_rows(key, part):
    base = shared_keys(key)
    return base.astype(jnp.bfloat16)


def draw_queries(key, part):
    key = jax.random.fold_in(key, 7)
    first = jax.random.fold_in(key, 0)
    drawn = jnp.clip(jax.random.normal(first, (TOKENS, HQ * HD), jnp.float32), -6.0, 6.0)
    return drawn.astype(jnp.bfloat16)


def draw_targets(key, part):
    key = jax.random.fold_in(key, 11)

    def column(column_key, seq_index):
        first, second, third, fourth = jax.random.split(column_key, 4)
        remaining = TOK_DEV - CAP
        base_count = remaining // (N_GRP - 1)
        extra_count = remaining % (N_GRP - 1)
        order = jax.random.permutation(first, N_GRP - 1)
        others = base_count + (order < extra_count).astype(jnp.int32)
        base_counts = jnp.concatenate([jnp.full((1,), CAP, jnp.int32), others.astype(jnp.int32)])
        rotate = jax.random.randint(second, (), 0, N_GRP)
        counts = base_counts[(jnp.arange(N_GRP, dtype=jnp.int32) - rotate) % N_GRP]
        ends = jnp.cumsum(counts).astype(jnp.int32)
        places = jnp.arange(TOK_DEV, dtype=jnp.int32)
        distance = jnp.sum((ends[None, :] <= places[:, None]).astype(jnp.int32), axis=1)
        sources = jnp.arange(N_GRP, dtype=jnp.int32)
        destination = (sources[:, None] + distance[None, :]) % N_GRP
        receive_perms = jax.vmap(lambda one_key: jax.random.permutation(one_key, TOK_DEV))(jax.random.split(third, N_GRP)).astype(jnp.int32)
        slots = receive_perms[destination, places[None, :]]
        values = destination * GROUP_LEN + seq_index * TOK_DEV + slots
        send_perms = jax.vmap(lambda one_key: jax.random.permutation(one_key, TOK_DEV))(jax.random.split(fourth, N_GRP))
        inverse = jnp.argsort(send_perms, axis=1)
        return jnp.take_along_axis(values, inverse, axis=1).astype(jnp.int32)
    columns = jax.vmap(column)(jax.random.split(key, N_SEQ), jnp.arange(N_SEQ, dtype=jnp.int32))
    return jnp.transpose(columns, (1, 0, 2)).reshape(-1).astype(jnp.int32)


def steps_of(rng, extent, cuts, low, top_value):
    gain = 1.0
    for dim, blocks in cuts:
        steps = jax.random.uniform(jax.random.fold_in(jax.random.fold_in(rng, 6), dim), (blocks,), jnp.float32, low / len(cuts), top_value / len(cuts))
        gain = gain * jnp.repeat(jnp.exp(steps), extent[dim] // blocks).reshape((-1,) + (1,) * (len(extent) - 1 - dim))
    return gain


def length_profile(amount, total, most, skew):
    loads = [(1 << 20) // math.isqrt(rank ** skew) + 1 for rank in range(2, amount + 1)]
    surplus, holding = total - most - (amount - 1), [1] * (amount - 1)
    while surplus > 0:
        candidates = [i for i in range(amount - 1) if holding[i] < most]
        pool, left = sum([loads[i] for i in candidates]), surplus
        for i in candidates:
            extra = min(most - holding[i], max(1, left * loads[i] // pool), surplus)
            holding[i] = holding[i] + extra
            surplus = surplus - extra
    return np.array([most] + holding)


def uneven_parts(own_key, number_of, total, most, skew):
    if number_of == 2:
        one = jax.random.randint(own_key, (), max(1, total - most), min(most, total - 1) + 1)
        return jnp.stack([one, total - one])
    tallies = jnp.asarray(length_profile(number_of, total, most, skew), jnp.int32)
    pairs = (number_of - 1) // 2
    source_of, receiver = tallies[1:1 + 2 * pairs:2], tallies[2:2 + 2 * pairs:2]
    room = jnp.minimum(source_of - 1, most - receiver)
    moved = jax.random.randint(jax.random.fold_in(own_key, 1), (pairs,), 0, 1 << 20) % (room + 1)
    tallies = tallies.at[1:1 + 2 * pairs:2].set(source_of - moved).at[2:2 + 2 * pairs:2].set(receiver + moved)
    return tallies[jax.random.permutation(jax.random.fold_in(own_key, 2), number_of)]


def scatter_about(stream_key, dims, deviation, limit, shards=(), kind=jnp.bfloat16):
    result = jax.random.normal(stream_key, dims, jnp.float32) * deviation
    if len(shards) > 0:
        result = steps_of(stream_key, dims, shards, -0.22, 0.18) * result
    return jnp.clip(result, min=-limit, max=limit).astype(kind)


def setup_inputs(seed: int = 0) -> dict:
    arg_keys = jax.random.split(jax.random.key(seed), 7)
    return {
        "queries": draw_queries(jax.random.fold_in(arg_keys[6], 71), 0),
        "key_rows": draw_key_rows(jax.random.fold_in(arg_keys[6], 71), 0),
        "value_rows": scatter_about(arg_keys[2], (TOKENS, KVH * HD), 1.0, 6.0, ((0, 256),)),
        "grad_rows": scatter_about(arg_keys[3], (TOKENS, HQ * HD), 1.0, 6.0, ((0, 256),)),
        "targets": draw_targets(jax.random.fold_in(arg_keys[6], 71), 0),
        "doc_lengths": jax.vmap(lambda own: uneven_parts(own, DOCS, GROUP_LEN, MAXDOC, 2))(jax.random.split(arg_keys[5], N_GRP)).reshape((N_GRP, DOCS)).astype(jnp.int32),
    }


def rounded(tensor):
    return lax.optimization_barrier(tensor.astype(jnp.bfloat16)).astype(jnp.float32)


def document_ids(lengths, count):
    ends = jnp.cumsum(lengths.astype(jnp.int32)).astype(jnp.int32)
    places = jnp.arange(count, dtype=jnp.int32)
    return jnp.sum((ends[None, :] <= places[:, None]).astype(jnp.int32), axis=1).astype(jnp.int32)


def block_pass(q_block, g_block, k_block, v_block, mask):
    highest = lax.Precision.HIGHEST
    scale = HD ** -0.5
    q_wide = q_block.astype(jnp.float32)
    g_wide = g_block.astype(jnp.float32)
    k_wide = k_block.astype(jnp.float32)
    v_wide = v_block.astype(jnp.float32)
    scores = jnp.einsum("rkgd,wkd->kgrw", q_wide, k_wide, precision=highest) * scale
    scores = jnp.where(mask, scores, -jnp.inf)
    top_score = jnp.max(scores, axis=-1, keepdims=True)
    powers = jnp.exp(scores - top_score)
    probs = powers / jnp.sum(powers, axis=-1, keepdims=True)
    probs_b = rounded(probs)
    attended = rounded(jnp.einsum("kgrw,wkd->rkgd", probs_b, v_wide, precision=highest))
    delta = jnp.sum(g_wide * attended, axis=-1)
    dprobs = jnp.einsum("rkgd,wkd->kgrw", g_wide, v_wide, precision=highest)
    dscores = rounded(probs * (dprobs - jnp.transpose(delta, (1, 2, 0))[..., None]))
    d_query = jnp.einsum("kgrw,wkd->rkgd", dscores, k_wide, precision=highest) * scale
    d_key = jnp.einsum("kgrw,rkgd->wkd", dscores, q_wide, precision=highest) * scale
    d_value = jnp.einsum("kgrw,rkgd->wkd", probs_b, g_wide, precision=highest)
    return d_query, d_key, d_value


def tile_sweep(query_blocks, grad_blocks, key_blocks, value_blocks, doc_ids):
    length = query_blocks.shape[0]
    kv_local = key_blocks.shape[1]
    width = MAXDOC + TILE
    pad_keys = jnp.concatenate([jnp.zeros((MAXDOC,) + key_blocks.shape[1:], key_blocks.dtype), key_blocks], axis=0)
    pad_values = jnp.concatenate([jnp.zeros((MAXDOC,) + value_blocks.shape[1:], value_blocks.dtype), value_blocks], axis=0)
    pad_ids = jnp.concatenate([jnp.full((MAXDOC,), -1, jnp.int32), doc_ids], axis=0)
    causal = (jnp.arange(width, dtype=jnp.int32)[None, :] - MAXDOC) <= jnp.arange(TILE, dtype=jnp.int32)[:, None]

    def advance(carry, index):
        key_sum, value_sum = carry
        start = index * TILE
        q_tile = lax.dynamic_slice_in_dim(query_blocks, start, TILE, 0)
        g_tile = lax.dynamic_slice_in_dim(grad_blocks, start, TILE, 0)
        k_tile = lax.dynamic_slice_in_dim(pad_keys, start, width, 0)
        v_tile = lax.dynamic_slice_in_dim(pad_values, start, width, 0)
        same_doc = lax.dynamic_slice_in_dim(pad_ids, start, width, 0)[None, :] == lax.dynamic_slice_in_dim(doc_ids, start, TILE, 0)[:, None]
        d_query, d_key, d_value = block_pass(q_tile, g_tile, k_tile, v_tile, causal & same_doc)
        key_sum = lax.dynamic_update_slice_in_dim(key_sum, lax.dynamic_slice_in_dim(key_sum, start, width, 0) + d_key, start, 0)
        value_sum = lax.dynamic_update_slice_in_dim(value_sum, lax.dynamic_slice_in_dim(value_sum, start, width, 0) + d_value, start, 0)
        return (key_sum, value_sum), d_query

    zero_sum = jnp.zeros((MAXDOC + length, kv_local, HD), jnp.float32)
    (key_sum, value_sum), tiles = lax.scan(advance, (zero_sum, zero_sum), jnp.arange(length // TILE, dtype=jnp.int32))
    return tiles.reshape((length, -1, HD)), key_sum[MAXDOC:], value_sum[MAXDOC:]


def reference(queries, key_rows, value_rows, grad_rows, targets, doc_lengths):
    def grouped(tensor):
        return jnp.zeros_like(tensor).at[targets].set(tensor)

    g_query = grouped(queries).reshape(N_GRP, GROUP_LEN, KVH, GQ, HD)
    g_grad = grouped(grad_rows).reshape(N_GRP, GROUP_LEN, KVH, GQ, HD)
    g_key = grouped(key_rows).reshape(N_GRP, GROUP_LEN, KVH, HD)
    g_value = grouped(value_rows).reshape(N_GRP, GROUP_LEN, KVH, HD)

    def one_group(operands):
        q_group, g_group, k_group, v_group, lengths = operands
        return tile_sweep(q_group, g_group, k_group, v_group, document_ids(lengths, GROUP_LEN))

    d_query, d_key, d_value = lax.map(one_group, (g_query, g_grad, g_key, g_value, doc_lengths))
    grad_query = d_query.reshape(TOKENS, HQ * HD)[targets].astype(jnp.bfloat16)
    grad_key = d_key.reshape(TOKENS, KVH * HD)[targets].astype(jnp.bfloat16)
    grad_value = d_value.reshape(TOKENS, KVH * HD)[targets].astype(jnp.bfloat16)
    return grad_query, grad_key, grad_value
```

```python
import functools

import jax
import jax.numpy as jnp
from jax import lax
from jax.experimental import pallas as pl
from jax.experimental.pallas import tpu as pltpu
from jax.sharding import PartitionSpec as P

HD = 128
KVH = 4
GQ = 16
DOCS = 16
ROWS = 128
CAP = 24
BACK = 4
WIN = (BACK + 1) * ROWS
STAGES = 2
PER = KVH // STAGES
CALLS = ((0, 2, 0, 0), (2, 1, 1, 0), (3, 1, 1, 1))
SUMS = ((0, 3), (3, 1))
WIDE = GQ * HD
SCALE = HD**-0.5
LOG2E = 1.4426950408889634
GROUPS = 8
FAR = 4
NEAR = (2, 3, 6, 7)
MSG = 2 * CAP
BSLOT = 64
PAIR = 256
A_PAIRS = GQ * ROWS // PAIR
B_PAIRS = GQ * BSLOT // PAIR
UNROLL = 4
f32, bf16, i32 = jnp.float32, jnp.bfloat16, jnp.int32
NT = (((1,), (1,)), ((), ()))


def dot(a, b, dims=None):
    if dims is None:
        return jnp.dot(a, b, preferred_element_type=f32)
    return lax.dot_general(a, b, dims, preferred_element_type=f32)


def iota(shape, dim):
    return lax.broadcasted_iota(i32, shape, dim)


def params(mib):
    return pltpu.CompilerParams(vmem_limit_bytes=mib * 1024 * 1024)


def arrival(group, hot, before, axis):
    if axis == 0:
        earlier = dot(hot.astype(bf16), before.astype(bf16))
    else:
        earlier = dot(before.astype(bf16), hot.astype(bf16))
    return jnp.sum(hot * earlier, axis=axis, keepdims=True).astype(i32)


def pack_keys(me_ref, length_ref, row_ref, col_ref, key_ref, value_ref, out_ref, order_ref, sort_ref):
    me = me_ref[0]
    group = row_ref[...] >> 12
    hot = (iota((GROUPS, ROWS), 0) == group).astype(f32)
    rank = arrival(group, hot, iota((ROWS, ROWS), 0) < iota((ROWS, ROWS), 1), 0)
    n = iota((GROUPS * MSG, ROWS), 0)
    both = (n == group * MSG + rank) | (n == (group ^ FAR) * MSG + CAP + rank)
    target = col_ref[...]
    group = target >> 12
    hot = (iota((ROWS, ROWS), 1) == group).astype(f32)
    rank = arrival(group, hot, iota((ROWS, ROWS), 1) < iota((ROWS, ROWS), 0), 1)
    order_ref[...] = (iota((ROWS, PAIR), 1) == (group ^ me) * CAP + rank).astype(bf16)
    n = iota((ROWS, GROUPS * MSG), 1)
    sort_ref[...] = ((n == group * MSG + rank) | (n == (group ^ FAR) * MSG + CAP + rank)).astype(bf16)
    lane = iota((1, HD), 1)
    slot = jnp.where(iota((ROWS, HD), 1) == 0, (target & (ROWS - 1)) + 1, 0).astype(f32).astype(bf16)
    extra = jnp.zeros((1, HD), i32)
    for k in range(DOCS):
        extra = jnp.where(lane == DOCS + k, length_ref[k] >> 8, extra)
        extra = jnp.where(lane == 2 * DOCS + k, length_ref[k] & 255, extra)
    parts = []
    for j in range(KVH):
        parts += [key_ref[:, j * HD : (j + 1) * HD], value_ref[:, j * HD : (j + 1) * HD]]
    packed = dot(both.astype(bf16), jnp.concatenate(parts + [slot], axis=1))
    out_ref[:, : KVH * 2 * HD] = packed[:, : KVH * 2 * HD].astype(bf16)
    out_ref[:, KVH * 2 * HD :] = (packed[:, KVH * 2 * HD :] + extra.astype(f32)).astype(bf16)


def pack_rows(me_ref, target_ref, mate_target_ref, query_ref, grad_ref, mate_query_ref, mate_grad_ref, _, *refs):
    outs, picks_ref = refs[:4], refs[4]

    @pl.when(pl.program_id(0) == 0)
    def _():
        for loader, ref in enumerate((target_ref, mate_target_ref)):
            group = ref[...] >> 12
            hot = (iota((GROUPS, ROWS), 0) == group).astype(f32)
            rank = arrival(group, hot, iota((ROWS, ROWS), 0) < iota((ROWS, ROWS), 1), 0)
            offset = group ^ me_ref[0]
            place = jnp.where((offset & 1) == 0, (offset >> 1) * MSG + loader * CAP + rank, -1)
            picks_ref[loader] = (iota((GROUPS * CAP, ROWS), 0) == place).astype(bf16)

    query = dot(picks_ref[0], query_ref[...]) + dot(picks_ref[1], mate_query_ref[...])
    grad = dot(picks_ref[0], grad_ref[...]) + dot(picks_ref[1], mate_grad_ref[...])
    for i, ref in enumerate(outs):
        at = slice(i * MSG, (i + 1) * MSG)
        ref[...] = jnp.concatenate([query[at], grad[at]], axis=0).astype(bf16)


def starts_of(lengths, position):
    before = (iota((HD, HD), 0) <= iota((HD, HD), 1)).astype(bf16)
    high, low = lengths
    ends = 256.0 * dot(high.astype(bf16), before) + dot(low.astype(bf16), before)
    ends = jnp.broadcast_to(ends[0:1], (ROWS, HD))
    held = (ends <= position.astype(f32)) & (iota((ROWS, HD), 1) < DOCS)
    return jnp.max(jnp.where(held, ends, 0.0), axis=1, keepdims=True)


def group_keys(me_ref, seq_ref, msg_ref, early_ref, late_ref, spread_ref, dense_ref, back_ref, vec_ref):
    wide = KVH * 2 * HD
    me = me_ref[0]
    first = (seq_ref[0] - BACK) * ROWS
    slot = msg_ref[:, wide : wide + 1].astype(f32)
    n, r = iota((GROUPS * MSG, ROWS), 0), iota((GROUPS * MSG, ROWS), 1)
    side_of = jnp.zeros_like(n)
    for k in range(GROUPS):
        side_of = jnp.where((n >= k * MSG + CAP) & (n < (k + 1) * MSG), 1, side_of)
    whole = []
    for side in range(2):
        hot = ((slot == (r + 1).astype(f32)) & (side_of == side)).astype(f32)
        spread_ref[side * GROUPS * MSG : (side + 1) * GROUPS * MSG, :] = hot.astype(bf16)
        whole.append(dot(jnp.transpose(hot).astype(bf16), msg_ref[:, :wide]).astype(bf16))
    for ref, at in ((early_ref, slice(0, wide // 2)), (late_ref, slice(wide // 2, wide))):
        ref[...] = jnp.concatenate([w[:, at] for w in whole], axis=0)

    def message(k):
        at = pl.multiple_of((me ^ k) * MSG, MSG)
        return msg_ref[pl.ds(at, MSG), wide : wide + HD].astype(f32)

    from_own, from_core = message(0), message(1)
    a_slots = [m[:CAP, :1] for m in [from_own, from_core] + [message(k) for k in NEAR]]
    twice = []
    for i in range(0, 6, 2):
        twice += a_slots[i : i + 2] * 2
    rows = 12 * CAP
    column = jnp.concatenate(twice + [jnp.zeros((384 - rows, 1), f32)], axis=0)
    lane = iota((384, 2 * ROWS), 1)
    n = iota((384, 2 * ROWS), 0)
    is_grad = jnp.zeros_like(n)
    for k in range(3):
        is_grad = jnp.where((n >= (2 * k + 1) * MSG) & (n < (2 * k + 2) * MSG), 1, is_grad)
    hot = (column == ((lane & (ROWS - 1)) + 1).astype(f32)) & (is_grad == (lane >> 7))
    dense_ref[...] = jnp.transpose(hot.astype(f32)).astype(bf16)
    column = jnp.concatenate(a_slots, axis=0)
    back_ref[...] = (column == (iota((6 * CAP, ROWS), 1) + 1).astype(f32)).astype(bf16)

    def lengths(rows):
        rows = jnp.broadcast_to(rows[:1], (8, HD))
        pick = (iota((HD, HD), 0) == iota((HD, HD), 1) + DOCS).astype(bf16)
        high = dot(rows.astype(bf16), pick)
        pick = (iota((HD, HD), 0) == iota((HD, HD), 1) + 2 * DOCS).astype(bf16)
        return high, dot(rows.astype(bf16), pick)

    row, column = iota((ROWS, ROWS), 0), iota((ROWS, ROWS), 1)
    position = iota((ROWS, 1), 0) + first + BACK * ROWS
    gap = jnp.zeros((BSLOT - 2 * CAP, 1), f32)
    half = [from_own[CAP:, :1], from_core[CAP:, :1], gap]
    arrived = jnp.concatenate(half + half, axis=0)
    hot_b = jnp.transpose((arrived == (column + 1).astype(f32)).astype(f32))
    hots = ((row == column).astype(f32), hot_b)
    for side in range(2):
        start = starts_of(lengths(from_own if side == 0 else message(FAR)), position) - first.astype(f32)
        low = jnp.sum(hots[side] * start, axis=0, keepdims=True)
        high = jnp.sum(hots[side] * (row + BACK * ROWS).astype(f32), axis=0, keepdims=True)
        vec_ref[2 * side : 2 * side + 1, :] = low.astype(i32)
        vec_ref[2 * side + 1 : 2 * side + 2, :] = high.astype(i32)
    vec_ref[4:8, :] = jnp.zeros((4, ROWS), i32)


def attend(x_ref, dense_ref, back_ref, vec_ref, *refs):
    ins, refs = refs[:4], refs[4:]
    window, refs = refs[: BACK + 1], refs[BACK + 1 :]
    refs = refs[len(refs) - 9 - 8 :]
    outs, refs = refs[:6], refs[6:]
    (sums_ref, far_ref), refs = refs[:2], refs[2:]
    bias_ref, q_ref, g_ref, dq_ref, key_ref, value_ref, flip_ref, dk_ref, dv_ref = refs

    @pl.when(pl.program_id(0) == 0)
    def _():
        c = iota((WIN, ROWS), 0)
        for side in range(2):
            low, high = vec_ref[2 * side : 2 * side + 1, :], vec_ref[2 * side + 1 : 2 * side + 2, :]
            bias = jnp.where((c >= low) & (c <= high), 0.0, -1e30).astype(f32)
            bias_ref[side, :, 0:ROWS] = bias
            bias_ref[side, :, ROWS : 2 * ROWS] = bias

    pieces = [r[...] for r in ins[:3]]
    pieces.append(jnp.zeros((384 - 12 * CAP, WIDE), bf16))
    rows_a = dot(dense_ref[...], jnp.concatenate(pieces, axis=0)).astype(bf16)
    gap = jnp.zeros((BSLOT - MSG, WIDE), bf16)
    rows_b = jnp.concatenate([ins[3][:MSG], gap, ins[3][MSG:], gap], axis=0)
    for h in range(GQ):
        at = slice(h * HD, (h + 1) * HD)
        q_ref[h * ROWS : (h + 1) * ROWS, :] = rows_a[:ROWS, at]
        g_ref[h * ROWS : (h + 1) * ROWS, :] = rows_a[ROWS:, at]
        to = GQ * ROWS + h * BSLOT
        q_ref[to : to + BSLOT, :] = rows_b[:BSLOT, at]
        g_ref[to : to + BSLOT, :] = rows_b[BSLOT:, at]

    for side in range(2):
        for k in range(BACK + 1):
            part = window[k][side * ROWS : (side + 1) * ROWS, :]
            key_ref[k * ROWS : (k + 1) * ROWS, :] = part[:, :HD]
            value_ref[k * ROWS : (k + 1) * ROWS, :] = part[:, HD:]
            flip_ref[:, k * ROWS : (k + 1) * ROWS] = jnp.transpose(part[:, :HD].astype(f32)).astype(bf16)
        dk_ref[...] = jnp.zeros_like(dk_ref)
        dv_ref[...] = jnp.zeros_like(dv_ref)

        def pair(step):
            at = pl.multiple_of((step + (A_PAIRS if side else 0)) * PAIR, PAIR)
            q, g = q_ref[pl.ds(at, PAIR), :], g_ref[pl.ds(at, PAIR), :]
            scores = dot(key_ref[...], q, NT) * (SCALE * LOG2E) + bias_ref[side]
            powers = jnp.exp2(scores - jnp.max(scores, axis=0, keepdims=True))
            probs = powers * (1.0 / jnp.sum(powers, axis=0, keepdims=True))
            dprobs = dot(value_ref[...], g, NT)
            weighted = probs * dprobs
            delta = jnp.sum(weighted, axis=0, keepdims=True)
            dscores = (weighted - probs * delta).astype(bf16)
            dv_ref[...] += dot(probs.astype(bf16), g)
            dk_ref[...] += dot(dscores, q)
            dq_ref[:, pl.ds(at, PAIR)] = (dot(flip_ref[...], dscores) * SCALE).astype(bf16)

        @pl.loop(0, (B_PAIRS if side else A_PAIRS) // UNROLL)
        def _(step):
            for u in range(UNROLL):
                pair(step * UNROLL + u)

        for k in range(BACK + 1):
            at = slice(k * ROWS, (k + 1) * ROWS)
            both = jnp.concatenate([dk_ref[at, :] * SCALE, dv_ref[at, :]], axis=1).astype(bf16)
            if k == 0:
                far_ref[side * ROWS : (side + 1) * ROWS, :] = both
            else:
                to = ((x_ref[0] + k) & 3) * (2 * ROWS) + side * ROWS
                sums_ref[pl.ds(pl.multiple_of(to, ROWS), ROWS), :] = both

    back = back_ref[...]
    eye = (iota((ROWS, ROWS), 0) == iota((ROWS, ROWS), 1)).astype(bf16)
    straight = []
    for i in range(GQ // 2):
        from_ = GQ * ROWS + i * ROWS
        straight.append(dot(eye, dq_ref[:, from_ : from_ + ROWS], NT))
    for h in range(GQ):
        at = slice(h * HD, (h + 1) * HD)
        rows = dot(back, dq_ref[:, h * ROWS : (h + 1) * ROWS], NT)
        low = h % 2 * BSLOT
        extra = straight[h // 2][low : low + 2 * CAP]
        outs[0][:, at] = jnp.concatenate([rows[:CAP], extra[:CAP]], axis=0).astype(bf16)
        outs[1][:, at] = jnp.concatenate([rows[CAP : 2 * CAP], extra[CAP:]], axis=0).astype(bf16)
        if h < GQ // 2:
            early = rows if h == 0 else jnp.concatenate([early, rows], axis=1)
        else:
            late = rows if h == GQ // 2 else jnp.concatenate([late, rows], axis=1)
    for k in range(4):
        at = slice((k + 2) * CAP, (k + 3) * CAP)
        outs[k + 2][...] = jnp.concatenate([early[at], late[at]], axis=0).astype(bf16)


def add_blocks(x_ref, ref, later):
    total = jnp.zeros((2 * ROWS, ref.shape[1]), f32)
    for j in range(4):
        weight = jnp.where((j >= x_ref[0]) == later, 1.0, 0.0).astype(f32)
        total = total + ref[j * 2 * ROWS : (j + 1) * 2 * ROWS, :].astype(f32) * weight
    return total


def pass_on(x_ref, sums_ref, far_ref, out_ref):
    out_ref[...] = (add_blocks(x_ref, sums_ref, False) + far_ref[...].astype(f32)).astype(bf16)


def return_keys(x_ref, spread_ref, *refs):
    ins, out_ref = refs[:-1], refs[-1]
    size = GROUPS * MSG
    for part, (first, count) in enumerate(SUMS):
        total = add_blocks(x_ref, ins[2 * part], True) + ins[2 * part + 1][...].astype(f32)
        total = total.astype(bf16)
        rows = dot(spread_ref[:size, :], total[:ROWS]) + dot(spread_ref[size:, :], total[ROWS:])
        out_ref[:, first * 2 * HD : (first + count) * 2 * HD] = rows.astype(bf16)


def unpack_keys(sort_ref, msg_ref, key_ref, value_ref):
    rows = dot(sort_ref[...], msg_ref[...]).astype(bf16)
    for j in range(KVH):
        key_ref[:, j * HD : (j + 1) * HD] = rows[:, 2 * j * HD : (2 * j + 1) * HD]
        value_ref[:, j * HD : (j + 1) * HD] = rows[:, (2 * j + 1) * HD : (2 * j + 2) * HD]


def unpack_rows(order_ref, own_ref, core_ref, *refs):
    near, out_ref = refs[:4], refs[-1]
    own, core = own_ref[...].astype(f32), core_ref[...].astype(f32)
    near = [r[...].astype(f32) for r in near]
    near = [jnp.concatenate([r[:CAP], r[CAP:]], axis=1) for r in near]
    rows = [own[:CAP], core[:CAP], near[0], near[1], own[CAP:], core[CAP:], near[2], near[3]]
    rows.append(jnp.zeros((PAIR - 8 * CAP, WIDE), f32))
    out_ref[...] = dot(order_ref[...], jnp.concatenate(rows, axis=0).astype(bf16)).astype(bf16)


def shape(*dims, dtype=bf16):
    return jax.ShapeDtypeStruct(dims, dtype)


def full(*dims):
    return pl.BlockSpec(dims, lambda *_: (0,) * len(dims))


def columns(rows, wide, first=0):
    return pl.BlockSpec((rows, wide), lambda i: (0, first + i))


SMEM = pl.BlockSpec(memory_space=pltpu.SMEM)


def cost(flops, size, powers=0):
    return pl.CostEstimate(flops=int(flops), bytes_accessed=int(size), transcendentals=int(powers))


def on_device(queries, key_rows, value_rows, grad_rows, targets, doc_lengths):
    seq_count = lax.axis_size("seq")
    me = lax.axis_index("grp").astype(i32).reshape(1)
    seq = lax.axis_index("seq").astype(i32).reshape(1)

    def swap(tensor, k):
        return lax.ppermute(tensor, "grp", [(i, i ^ k) for i in range(GROUPS)])

    def later(tensor, distance):
        return lax.ppermute(tensor, "seq", [(i, (i + distance) % seq_count) for i in range(seq_count)])

    def earlier(tensor, distance):
        return lax.ppermute(tensor, "seq", [((i + distance) % seq_count, i) for i in range(seq_count)])

    wide = KVH * 2 * HD
    message, order, sort = pl.pallas_call(
        pack_keys,
        out_shape=[
            shape(GROUPS * MSG, wide + HD),
            shape(ROWS, PAIR),
            shape(ROWS, GROUPS * MSG),
        ],
        in_specs=[SMEM] * 2 + [pl.BlockSpec(memory_space=pltpu.VMEM)] * 4,
        compiler_params=params(32),
        cost_estimate=cost(1e8, 1 << 20),
        name="pack_keys",
    )(me, doc_lengths[0], targets.reshape(1, ROWS), targets.reshape(ROWS, 1), key_rows, value_rows)
    message = lax.all_to_all(message, "grp", split_axis=0, concat_axis=0, tiled=True)

    step = 1024
    mate_target = swap(targets, 1)
    mate_query, mate_grad = swap(queries, 1), swap(grad_rows, 1)
    packed = pl.pallas_call(
        pack_rows,
        grid=(KVH * WIDE // step,),
        out_shape=[shape(2 * MSG, KVH * WIDE)] * 4,
        in_specs=[SMEM] + [full(1, ROWS)] * 2 + [columns(ROWS, step)] * 4 + [pl.BlockSpec(memory_space=pl.ANY)],
        out_specs=[columns(2 * MSG, step)] * 4,
        scratch_shapes=[pltpu.VMEM((2, GROUPS * CAP, ROWS), bf16)],
        compiler_params=params(60),
        cost_estimate=cost(8e8, 10 << 20),
        name="pack_rows",
    )(me, targets.reshape(1, ROWS), mate_target.reshape(1, ROWS), queries, grad_rows, mate_query, mate_grad, order)
    near, far, message = lax.optimization_barrier((packed[1], packed[3], message))
    pieces = [packed[0], swap(near, 2), swap(far, 6), packed[2]]

    *own, spread, dense, back, vec = pl.pallas_call(
        group_keys,
        out_shape=[
            shape(2 * ROWS, wide // 2),
            shape(2 * ROWS, wide // 2),
            shape(2 * GROUPS * MSG, ROWS),
            shape(2 * ROWS, 384),
            shape(6 * CAP, ROWS),
            shape(8, ROWS, dtype=i32),
        ],
        in_specs=[SMEM] * 2 + [pl.BlockSpec(memory_space=pltpu.VMEM)],
        compiler_params=params(32),
        cost_estimate=cost(2e8, 2 << 20),
        name="group_keys",
    )(me, seq, message)

    windows = [[later(part, d) for d in range(BACK, 0, -1)] + [part] for part in own]
    x = seq & 3
    lanes = GQ * (ROWS + BSLOT)
    rows, sums, partial, gradients = {}, {}, {}, {}

    def unpack(stage, grad_query):
        operands = [order, *gradients[stage]]
        in_specs = [full(ROWS, PAIR)] + [columns(2 * CAP, WIDE)] * 2 + [columns(2 * CAP, WIDE // 2)] * 4
        aliases = {}
        if grad_query is not None:
            operands.append(grad_query)
            in_specs.append(pl.BlockSpec(memory_space=pl.ANY))
            aliases = {len(operands) - 1: 0}
        return pl.pallas_call(
            unpack_rows,
            grid=(PER,),
            out_shape=shape(ROWS, KVH * WIDE),
            in_specs=in_specs,
            out_specs=columns(ROWS, WIDE, stage * PER),
            input_output_aliases=aliases,
            compiler_params=params(60),
            cost_estimate=cost(2e8, 3 << 20),
            name="unpack_rows",
        )(*operands)

    for call, (first, count, stage, part) in enumerate(CALLS):
        row_at, (sum_first, sum_count) = first - stage * PER, SUMS[part]
        operands = [x, dense, back, vec, *pieces, *windows[stage]]
        fixed = len(operands)
        aliases, outputs = {}, 0
        for begun, size in ((rows.get(stage), 6), (sums.get(part), 2)):
            for i, array in enumerate(begun or ()):
                aliases[len(operands)] = outputs + i
                operands.append(array)
            outputs += size
        if call == len(CALLS) - 1:
            operands += gradients[0][1:]
        result = pl.pallas_call(
            attend,
            grid=(count,),
            out_shape=[shape(2 * CAP, PER * WIDE)] * 2
            + [shape(2 * CAP, PER * WIDE // 2)] * 4
            + [shape(8 * ROWS, sum_count * 2 * HD), shape(2 * ROWS, sum_count * 2 * HD)],
            in_specs=[SMEM, full(2 * ROWS, 384), full(6 * CAP, ROWS), full(8, ROWS)]
            + [columns(2 * MSG, WIDE, first)] * 4
            + [columns(2 * ROWS, 2 * HD, row_at)] * (BACK + 1)
            + [pl.BlockSpec(memory_space=pl.ANY)] * (len(operands) - fixed),
            out_specs=[columns(2 * CAP, WIDE, row_at)] * 2
            + [columns(2 * CAP, WIDE // 2, row_at)] * 4
            + [columns(r * ROWS, 2 * HD, first - sum_first) for r in (8, 2)],
            input_output_aliases=aliases,
            scratch_shapes=[
                pltpu.VMEM((2, WIN, 2 * ROWS), f32),
                pltpu.VMEM((lanes, HD), bf16),
                pltpu.VMEM((lanes, HD), bf16),
                pltpu.VMEM((HD, lanes), bf16),
                pltpu.VMEM((WIN, HD), bf16),
                pltpu.VMEM((WIN, HD), bf16),
                pltpu.VMEM((HD, WIN), bf16),
                pltpu.VMEM((WIN, HD), f32),
                pltpu.VMEM((WIN, HD), f32),
            ],
            compiler_params=params(60),
            cost_estimate=cost(count * lanes * WIN * HD * 2 * 10, 8 << 20, count * lanes * WIN),
            name="attend",
        )(*operands)
        rows[stage], sums[part] = result[:6], result[6:]
        if call + 1 == len(CALLS) or CALLS[call + 1][2] != stage:
            done = rows[stage]
            gradients[stage] = [done[0]] + [swap(p, k) for p, k in zip(done[1:], (1,) + NEAR)]
        if call + 1 == len(CALLS) or CALLS[call + 1][3] != part:
            terms, far = sums[part]
            rings = [[4 * z + i for i in range(4)] for z in range(seq_count // 4)]
            terms = lax.all_to_all(
                terms, "seq", split_axis=0, concat_axis=0, axis_index_groups=rings, tiled=True
            )
            partial[part] = [terms, far]

    for part, (_, count) in enumerate(SUMS):
        terms, far = partial[part]
        held = partial[len(SUMS) - 1][1] if part + 1 < len(SUMS) else (gradients[1][2], gradients[1][4])
        terms, _ = lax.optimization_barrier((terms, held))
        rest = pl.pallas_call(
            pass_on,
            out_shape=shape(2 * ROWS, count * 2 * HD),
            in_specs=[SMEM] + [pl.BlockSpec(memory_space=pltpu.VMEM)] * 2,
            compiler_params=params(32),
            cost_estimate=cost(1e6, 2 << 20),
            name="pass_on",
        )(x, terms, far)
        partial[part] = [terms, earlier(rest, BACK)]

    spread, _ = lax.optimization_barrier((spread, (gradients[1][1], gradients[1][3], gradients[1][5])))
    message = pl.pallas_call(
        return_keys,
        out_shape=shape(GROUPS * MSG, wide),
        compiler_params=params(32),
        in_specs=[SMEM] + [pl.BlockSpec(memory_space=pltpu.VMEM)] * (1 + 2 * len(SUMS)),
        cost_estimate=cost(1e8, 3 << 20),
        name="return_keys",
    )(x, spread, *partial[0], *partial[1])
    message = lax.all_to_all(message, "grp", split_axis=0, concat_axis=0, tiled=True)

    grad_query = unpack(1, unpack(0, None))

    grad_key, grad_value = pl.pallas_call(
        unpack_keys,
        out_shape=[shape(ROWS, KVH * HD)] * 2,
        compiler_params=params(32),
        cost_estimate=cost(1e8, 1 << 20),
        name="unpack_keys",
    )(sort, message)
    return (grad_query, grad_key, grad_value)


def solution(mesh):
    in_specs = (
        P(("grp", "seq"), None),
        P(("grp", "seq"), None),
        P(("grp", "seq"), None),
        P(("grp", "seq"), None),
        P(("grp", "seq")),
        P("grp", None),
    )
    out_specs = (P(("grp", "seq"), None), P(("grp", "seq"), None), P(("grp", "seq"), None))
    return jax.shard_map(
        on_device, mesh=mesh, in_specs=in_specs, out_specs=out_specs, check_vma=False
    )
```

```python
import functools

import jax
import jax.numpy as jnp
from jax import lax
from jax.experimental import pallas as pl
from jax.experimental.pallas import tpu as pltpu
from jax.sharding import PartitionSpec as P

HD = 128
KVH = 4
GQ = 16
DOCS = 16
ROWS = 128
CAP = 24
BACK = 4
WIN = (BACK + 1) * ROWS
EARLY = 2
CALLS = ((0, EARLY, 0), (EARLY, KVH - EARLY, 1))
SUMS = ((0, EARLY), (EARLY, KVH - EARLY))
WIDE = GQ * HD
SCALE = HD**-0.5
LOG2E = 1.4426950408889634
GROUPS = 8
FAR = 4
NEAR = (2, 3, 6, 7)
MSG = 2 * CAP
BSLOT = 64
PAIR = 256
A_PAIRS = GQ * ROWS // PAIR
B_PAIRS = GQ * BSLOT // PAIR
UNROLL = 4
f32, bf16, i32 = jnp.float32, jnp.bfloat16, jnp.int32
NT = (((1,), (1,)), ((), ()))


def dot(a, b, dims=None):
    if dims is None:
        return jnp.dot(a, b, preferred_element_type=f32)
    return lax.dot_general(a, b, dims, preferred_element_type=f32)


def iota(shape, dim):
    return lax.broadcasted_iota(i32, shape, dim)


def params(mib):
    return pltpu.CompilerParams(vmem_limit_bytes=mib * 1024 * 1024)


def arrival(group, hot, before, axis):
    if axis == 0:
        earlier = dot(hot.astype(bf16), before.astype(bf16))
    else:
        earlier = dot(before.astype(bf16), hot.astype(bf16))
    return jnp.sum(hot * earlier, axis=axis, keepdims=True).astype(i32)


def pack_keys(me_ref, length_ref, row_ref, col_ref, key_ref, value_ref, out_ref, order_ref, sort_ref):
    me = me_ref[0]
    group = row_ref[...] >> 12
    hot = (iota((GROUPS, ROWS), 0) == group).astype(f32)
    rank = arrival(group, hot, iota((ROWS, ROWS), 0) < iota((ROWS, ROWS), 1), 0)
    n = iota((GROUPS * MSG, ROWS), 0)
    both = (n == group * MSG + rank) | (n == (group ^ FAR) * MSG + CAP + rank)
    target = col_ref[...]
    group = target >> 12
    hot = (iota((ROWS, ROWS), 1) == group).astype(f32)
    rank = arrival(group, hot, iota((ROWS, ROWS), 1) < iota((ROWS, ROWS), 0), 1)
    order_ref[...] = (iota((ROWS, PAIR), 1) == (group ^ me) * CAP + rank).astype(bf16)
    n = iota((ROWS, GROUPS * MSG), 1)
    sort_ref[...] = ((n == group * MSG + rank) | (n == (group ^ FAR) * MSG + CAP + rank)).astype(bf16)
    lane = iota((1, HD), 1)
    slot = jnp.where(iota((ROWS, HD), 1) == 0, (target & (ROWS - 1)) + 1, 0).astype(f32).astype(bf16)
    extra = jnp.zeros((1, HD), i32)
    for k in range(DOCS):
        extra = jnp.where(lane == DOCS + k, length_ref[k] >> 8, extra)
        extra = jnp.where(lane == 2 * DOCS + k, length_ref[k] & 255, extra)
    parts = []
    for j in range(KVH):
        parts += [key_ref[:, j * HD : (j + 1) * HD], value_ref[:, j * HD : (j + 1) * HD]]
    packed = dot(both.astype(bf16), jnp.concatenate(parts + [slot], axis=1))
    out_ref[:, : KVH * 2 * HD] = packed[:, : KVH * 2 * HD].astype(bf16)
    out_ref[:, KVH * 2 * HD :] = (packed[:, KVH * 2 * HD :] + extra.astype(f32)).astype(bf16)


def pack_rows(blocks, me_ref, target_ref, mate_target_ref, query_ref, grad_ref, mate_query_ref, mate_grad_ref, _, *refs):
    outs, picks_ref = refs[:-1], refs[-1]
    @pl.when(pl.program_id(0) == 0)
    def _():
        for loader, ref in enumerate((target_ref, mate_target_ref)):
            group = ref[...] >> 12
            hot = (iota((GROUPS, ROWS), 0) == group).astype(f32)
            rank = arrival(group, hot, iota((ROWS, ROWS), 0) < iota((ROWS, ROWS), 1), 0)
            offset = group ^ me_ref[0]
            place = jnp.where((offset & 1) == 0, (offset >> 1) * MSG + loader * CAP + rank, -1)
            picks_ref[loader] = (iota((GROUPS * CAP, ROWS), 0) == place).astype(bf16)

    picks = [
        jnp.concatenate([picks_ref[loader, i * MSG : (i + 1) * MSG, :] for i in blocks], axis=0)
        for loader in range(2)
    ]
    query = dot(picks[0], query_ref[...]) + dot(picks[1], mate_query_ref[...])
    grad = dot(picks[0], grad_ref[...]) + dot(picks[1], mate_grad_ref[...])
    for i, ref in enumerate(outs):
        at = slice(i * MSG, (i + 1) * MSG)
        ref[...] = jnp.concatenate([query[at], grad[at]], axis=0).astype(bf16)


def starts_of(lengths, position):
    before = (iota((HD, HD), 0) <= iota((HD, HD), 1)).astype(bf16)
    high, low = lengths
    ends = 256.0 * dot(high.astype(bf16), before) + dot(low.astype(bf16), before)
    ends = jnp.broadcast_to(ends[0:1], (ROWS, HD))
    held = (ends <= position.astype(f32)) & (iota((ROWS, HD), 1) < DOCS)
    return jnp.max(jnp.where(held, ends, 0.0), axis=1, keepdims=True)


def group_keys(me_ref, seq_ref, msg_ref, whole_ref, early_ref, late_ref, spread_ref, dense_ref, back_ref, vec_ref):
    wide = KVH * 2 * HD
    me = me_ref[0]
    first = (seq_ref[0] - BACK) * ROWS
    slot = msg_ref[:, wide : wide + 1].astype(f32)
    n, r = iota((GROUPS * MSG, ROWS), 0), iota((GROUPS * MSG, ROWS), 1)
    side_of = jnp.zeros_like(n)
    for k in range(GROUPS):
        side_of = jnp.where((n >= k * MSG + CAP) & (n < (k + 1) * MSG), 1, side_of)
    whole = []
    for side in range(2):
        hot = ((slot == (r + 1).astype(f32)) & (side_of == side)).astype(f32)
        spread_ref[side * GROUPS * MSG : (side + 1) * GROUPS * MSG, :] = hot.astype(bf16)
        whole.append(dot(jnp.transpose(hot).astype(bf16), msg_ref[:, :wide]).astype(bf16))
    whole_ref[...] = jnp.concatenate(whole, axis=0)
    for ref, at in ((early_ref, slice(0, EARLY * 2 * HD)), (late_ref, slice(EARLY * 2 * HD, wide))):
        ref[...] = jnp.concatenate([w[:, at] for w in whole], axis=0)

    def message(k):
        at = pl.multiple_of((me ^ k) * MSG, MSG)
        return msg_ref[pl.ds(at, MSG), wide : wide + HD].astype(f32)

    from_own, from_core = message(0), message(1)
    a_slots = [m[:CAP, :1] for m in [from_own, from_core] + [message(k) for k in NEAR]]
    twice = []
    for i in range(0, 6, 2):
        twice += a_slots[i : i + 2] * 2
    rows = 12 * CAP
    column = jnp.concatenate(twice + [jnp.zeros((384 - rows, 1), f32)], axis=0)
    lane = iota((384, 2 * ROWS), 1)
    n = iota((384, 2 * ROWS), 0)
    is_grad = jnp.zeros_like(n)
    for k in range(3):
        is_grad = jnp.where((n >= (2 * k + 1) * MSG) & (n < (2 * k + 2) * MSG), 1, is_grad)
    hot = (column == ((lane & (ROWS - 1)) + 1).astype(f32)) & (is_grad == (lane >> 7))
    dense_ref[...] = jnp.transpose(hot.astype(f32)).astype(bf16)
    column = jnp.concatenate(a_slots, axis=0)
    back_ref[...] = (column == (iota((6 * CAP, ROWS), 1) + 1).astype(f32)).astype(bf16)

    def lengths(rows):
        rows = jnp.broadcast_to(rows[:1], (8, HD))
        pick = (iota((HD, HD), 0) == iota((HD, HD), 1) + DOCS).astype(bf16)
        high = dot(rows.astype(bf16), pick)
        pick = (iota((HD, HD), 0) == iota((HD, HD), 1) + 2 * DOCS).astype(bf16)
        return high, dot(rows.astype(bf16), pick)

    row, column = iota((ROWS, ROWS), 0), iota((ROWS, ROWS), 1)
    position = iota((ROWS, 1), 0) + first + BACK * ROWS
    gap = jnp.zeros((BSLOT - 2 * CAP, 1), f32)
    half = [from_own[CAP:, :1], from_core[CAP:, :1], gap]
    arrived = jnp.concatenate(half + half, axis=0)
    hot_b = jnp.transpose((arrived == (column + 1).astype(f32)).astype(f32))
    hots = ((row == column).astype(f32), hot_b)
    for side in range(2):
        start = starts_of(lengths(from_own if side == 0 else message(FAR)), position) - first.astype(f32)
        low = jnp.sum(hots[side] * start, axis=0, keepdims=True)
        high = jnp.sum(hots[side] * (row + BACK * ROWS).astype(f32), axis=0, keepdims=True)
        vec_ref[2 * side : 2 * side + 1, :] = low.astype(i32)
        vec_ref[2 * side + 1 : 2 * side + 2, :] = high.astype(i32)
    vec_ref[4:8, :] = jnp.zeros((4, ROWS), i32)


def attend(x_ref, dense_ref, back_ref, vec_ref, *refs):
    ins, refs = refs[:4], refs[4:]
    window, refs = refs[: BACK + 1], refs[BACK + 1 :]
    refs = refs[len(refs) - 9 - 8 :]
    outs, refs = refs[:6], refs[6:]
    (sums_ref, far_ref), refs = refs[:2], refs[2:]
    bias_ref, q_ref, g_ref, dq_ref, key_ref, value_ref, flip_ref, dk_ref, dv_ref = refs

    @pl.when(pl.program_id(0) == 0)
    def _():
        c = iota((WIN, ROWS), 0)
        for side in range(2):
            low, high = vec_ref[2 * side : 2 * side + 1, :], vec_ref[2 * side + 1 : 2 * side + 2, :]
            bias = jnp.where((c >= low) & (c <= high), 0.0, -1e30).astype(f32)
            bias_ref[side, :, 0:ROWS] = bias
            bias_ref[side, :, ROWS : 2 * ROWS] = bias

    pieces = [r[...] for r in ins[:3]]
    pieces.append(jnp.zeros((384 - 12 * CAP, WIDE), bf16))
    rows_a = dot(dense_ref[...], jnp.concatenate(pieces, axis=0)).astype(bf16)
    gap = jnp.zeros((BSLOT - MSG, WIDE), bf16)
    rows_b = jnp.concatenate([ins[3][:MSG], gap, ins[3][MSG:], gap], axis=0)
    for h in range(GQ):
        at = slice(h * HD, (h + 1) * HD)
        q_ref[h * ROWS : (h + 1) * ROWS, :] = rows_a[:ROWS, at]
        g_ref[h * ROWS : (h + 1) * ROWS, :] = rows_a[ROWS:, at]
        to = GQ * ROWS + h * BSLOT
        q_ref[to : to + BSLOT, :] = rows_b[:BSLOT, at]
        g_ref[to : to + BSLOT, :] = rows_b[BSLOT:, at]

    for side in range(2):
        for k in range(BACK + 1):
            part = window[k][side * ROWS : (side + 1) * ROWS, :]
            key_ref[k * ROWS : (k + 1) * ROWS, :] = part[:, :HD]
            value_ref[k * ROWS : (k + 1) * ROWS, :] = part[:, HD:]
            flip_ref[:, k * ROWS : (k + 1) * ROWS] = jnp.transpose(part[:, :HD].astype(f32)).astype(bf16)
        dk_ref[...] = jnp.zeros_like(dk_ref)
        dv_ref[...] = jnp.zeros_like(dv_ref)

        def pair(at):
            q, g = q_ref[pl.ds(at, PAIR), :], g_ref[pl.ds(at, PAIR), :]
            scores = dot(key_ref[...], q, NT) * (SCALE * LOG2E) + bias_ref[side]
            powers = jnp.exp2(scores - jnp.max(scores, axis=0, keepdims=True))
            probs = powers * (1.0 / jnp.sum(powers, axis=0, keepdims=True))
            dprobs = dot(value_ref[...], g, NT)
            weighted = probs * dprobs
            delta = jnp.sum(weighted, axis=0, keepdims=True)
            return probs.astype(bf16), (weighted - probs * delta).astype(bf16)

        @pl.loop(0, (B_PAIRS if side else A_PAIRS) // UNROLL)
        def _(step):
            wide = UNROLL * PAIR
            at = pl.multiple_of(step * wide + (A_PAIRS * PAIR if side else 0), PAIR)
            parts = [pair(at + u * PAIR) for u in range(UNROLL)]
            probs = jnp.concatenate([p for p, _ in parts], axis=1)
            dscores = jnp.concatenate([d for _, d in parts], axis=1)
            dv_ref[...] += dot(probs, g_ref[pl.ds(at, wide), :])
            dk_ref[...] += dot(dscores, q_ref[pl.ds(at, wide), :])
            dq_ref[:, pl.ds(at, wide)] = (dot(flip_ref[...], dscores) * SCALE).astype(bf16)

        for k in range(BACK + 1):
            at = slice(k * ROWS, (k + 1) * ROWS)
            both = jnp.concatenate([dk_ref[at, :] * SCALE, dv_ref[at, :]], axis=1).astype(bf16)
            if k == 0:
                far_ref[side * ROWS : (side + 1) * ROWS, :] = both
            else:
                to = ((x_ref[0] + k) & 3) * (2 * ROWS) + side * ROWS
                sums_ref[pl.ds(pl.multiple_of(to, ROWS), ROWS), :] = both

    back = back_ref[...]
    eye = (iota((ROWS, ROWS), 0) == iota((ROWS, ROWS), 1)).astype(bf16)
    straight = []
    for i in range(GQ // 2):
        from_ = GQ * ROWS + i * ROWS
        straight.append(dot(eye, dq_ref[:, from_ : from_ + ROWS], NT))
    for h in range(GQ):
        at = slice(h * HD, (h + 1) * HD)
        rows = dot(back, dq_ref[:, h * ROWS : (h + 1) * ROWS], NT)
        low = h % 2 * BSLOT
        extra = straight[h // 2][low : low + 2 * CAP]
        outs[0][:, at] = jnp.concatenate([rows[:CAP], extra[:CAP]], axis=0).astype(bf16)
        outs[1][:, at] = jnp.concatenate([rows[CAP : 2 * CAP], extra[CAP:]], axis=0).astype(bf16)
        if h < GQ // 2:
            early = rows if h == 0 else jnp.concatenate([early, rows], axis=1)
        else:
            late = rows if h == GQ // 2 else jnp.concatenate([late, rows], axis=1)
    for k in range(4):
        at = slice((k + 2) * CAP, (k + 3) * CAP)
        outs[k + 2][...] = jnp.concatenate([early[at], late[at]], axis=0).astype(bf16)


def add_blocks(x_ref, ref, later):
    total = jnp.zeros((2 * ROWS, ref.shape[1]), f32)
    for j in range(4):
        weight = jnp.where((j >= x_ref[0]) == later, 1.0, 0.0).astype(f32)
        total = total + ref[j * 2 * ROWS : (j + 1) * 2 * ROWS, :].astype(f32) * weight
    return total


def pass_on(x_ref, sums_ref, far_ref, out_ref):
    out_ref[...] = (add_blocks(x_ref, sums_ref, False) + far_ref[...].astype(f32)).astype(bf16)


def return_keys(x_ref, spread_ref, *refs):
    ins, out_ref = refs[:-1], refs[-1]
    size = GROUPS * MSG
    for part, (first, count) in enumerate(SUMS):
        total = add_blocks(x_ref, ins[2 * part], True) + ins[2 * part + 1][...].astype(f32)
        total = total.astype(bf16)
        rows = dot(spread_ref[:size, :], total[:ROWS]) + dot(spread_ref[size:, :], total[ROWS:])
        out_ref[:, first * 2 * HD : (first + count) * 2 * HD] = rows.astype(bf16)


def unpack_keys(sort_ref, msg_ref, key_ref, value_ref):
    rows = dot(sort_ref[...], msg_ref[...]).astype(bf16)
    for j in range(KVH):
        key_ref[:, j * HD : (j + 1) * HD] = rows[:, 2 * j * HD : (2 * j + 1) * HD]
        value_ref[:, j * HD : (j + 1) * HD] = rows[:, (2 * j + 1) * HD : (2 * j + 2) * HD]


def unpack_rows(order_ref, own_ref, core_ref, *refs):
    near, out_ref = refs[:4], refs[-1]
    own, core = own_ref[...].astype(f32), core_ref[...].astype(f32)
    near = [r[...].astype(f32) for r in near]
    near = [jnp.concatenate([r[:CAP], r[CAP:]], axis=1) for r in near]
    rows = [own[:CAP], core[:CAP], near[0], near[1], own[CAP:], core[CAP:], near[2], near[3]]
    rows.append(jnp.zeros((PAIR - 8 * CAP, WIDE), f32))
    out_ref[...] = dot(order_ref[...], jnp.concatenate(rows, axis=0).astype(bf16)).astype(bf16)


def shape(*dims, dtype=bf16):
    return jax.ShapeDtypeStruct(dims, dtype)


def full(*dims):
    return pl.BlockSpec(dims, lambda *_: (0,) * len(dims))


def columns(rows, wide, first=0):
    return pl.BlockSpec((rows, wide), lambda i: (0, first + i))


SMEM = pl.BlockSpec(memory_space=pltpu.SMEM)


def cost(flops, size, powers=0):
    return pl.CostEstimate(flops=int(flops), bytes_accessed=int(size), transcendentals=int(powers))


def on_device(queries, key_rows, value_rows, grad_rows, targets, doc_lengths):
    seq_count = lax.axis_size("seq")
    me = lax.axis_index("grp").astype(i32).reshape(1)
    seq = lax.axis_index("seq").astype(i32).reshape(1)

    def swap(tensor, k):
        return lax.ppermute(tensor, "grp", [(i, i ^ k) for i in range(GROUPS)])

    def later(tensor, distance):
        return lax.ppermute(tensor, "seq", [(i, (i + distance) % seq_count) for i in range(seq_count)])

    def earlier(tensor, distance):
        return lax.ppermute(tensor, "seq", [((i + distance) % seq_count, i) for i in range(seq_count)])

    wide = KVH * 2 * HD
    message, order, sort = pl.pallas_call(
        pack_keys,
        out_shape=[
            shape(GROUPS * MSG, wide + HD),
            shape(ROWS, PAIR),
            shape(ROWS, GROUPS * MSG),
        ],
        in_specs=[SMEM] * 2 + [pl.BlockSpec(memory_space=pltpu.VMEM)] * 4,
        compiler_params=params(32),
        cost_estimate=cost(1e8, 1 << 20),
        name="pack_keys",
    )(me, doc_lengths[0], targets.reshape(1, ROWS), targets.reshape(ROWS, 1), key_rows, value_rows)
    message = lax.all_to_all(message, "grp", split_axis=0, concat_axis=0, tiled=True)

    step = 1024
    mate_target = swap(targets, 1)
    mate_query, mate_grad = swap(queries, 1), swap(grad_rows, 1)
    def pack(blocks, first, count, after):
        return pl.pallas_call(
            functools.partial(pack_rows, blocks),
            grid=(count * WIDE // step,),
            out_shape=[shape(2 * MSG, count * WIDE)] * len(blocks),
            in_specs=[SMEM]
            + [full(1, ROWS)] * 2
            + [columns(ROWS, step, first * (WIDE // step))] * 4
            + [pl.BlockSpec(memory_space=pl.ANY)],
            out_specs=[columns(2 * MSG, step)] * len(blocks),
            scratch_shapes=[pltpu.VMEM((2, GROUPS * CAP, ROWS), bf16)],
            compiler_params=params(60),
            cost_estimate=cost(count * 1e8, count * 2 << 20),
            name="pack_rows",
        )(me, targets.reshape(1, ROWS), mate_target.reshape(1, ROWS), queries, grad_rows, mate_query, mate_grad, after)

    early = pack((1, 3), 0, EARLY, order)
    late = pack((1, 3), EARLY, KVH - EARLY, order)
    *rows, message = lax.optimization_barrier((*early, *late, message))
    early, late = rows[:2], rows[2:]
    early = [swap(early[0], 2), swap(early[1], 6)]

    whole, *own, spread, dense, back, vec = pl.pallas_call(
        group_keys,
        out_shape=[
            shape(2 * ROWS, wide),
            shape(2 * ROWS, EARLY * 2 * HD),
            shape(2 * ROWS, wide - EARLY * 2 * HD),
            shape(2 * GROUPS * MSG, ROWS),
            shape(2 * ROWS, 384),
            shape(6 * CAP, ROWS),
            shape(8, ROWS, dtype=i32),
        ],
        in_specs=[SMEM] * 2 + [pl.BlockSpec(memory_space=pltpu.VMEM)],
        compiler_params=params(32),
        cost_estimate=cost(2e8, 2 << 20),
        name="group_keys",
    )(me, seq, message)

    x = seq & 3
    whole = later(whole, 3)
    windows = []
    for stage, part in enumerate(own):
        window = {d: later(part, d) for d in (4, 2, 1)}
        window[0] = part
        window[3] = whole
        windows.append([window[d] for d in range(BACK, -1, -1)])
        if stage == 0:
            late = lax.optimization_barrier((*late, *early, part))[:2]
            late = [swap(late[0], 2), swap(late[1], 6)]
    lanes = GQ * (ROWS + BSLOT)
    rows, sums, partial = None, {}, {}
    for first, count, part in CALLS:
        stage, row_at, (sum_first, sum_count) = part, 0, SUMS[part]
        here = pack((0, 2), first, count, order if rows is None else rows[0])
        operands = [x, dense, back, vec, here[0], *(late if stage else early), here[1], *windows[stage]]
        fixed = len(operands)
        aliases, outputs = {}, 0
        for begun, size in ((rows, 6), (sums.get(part), 2)):
            for i, array in enumerate(begun or ()):
                aliases[len(operands)] = outputs + i
                operands.append(array)
            outputs += size
        result = pl.pallas_call(
            attend,
            grid=(count,),
            out_shape=[shape(2 * CAP, KVH * WIDE)] * 2
            + [shape(2 * CAP, KVH * WIDE // 2)] * 4
            + [shape(8 * ROWS, sum_count * 2 * HD), shape(2 * ROWS, sum_count * 2 * HD)],
            in_specs=[SMEM, full(2 * ROWS, 384), full(6 * CAP, ROWS), full(8, ROWS)]
            + [columns(2 * MSG, WIDE, at) for at in (row_at,) * 4]
            + [columns(2 * ROWS, 2 * HD, first if d == 3 else row_at) for d in range(BACK, -1, -1)]
            + [pl.BlockSpec(memory_space=pl.ANY)] * (len(operands) - fixed),
            out_specs=[columns(2 * CAP, WIDE, first)] * 2
            + [columns(2 * CAP, WIDE // 2, first)] * 4
            + [columns(r * ROWS, 2 * HD, first - sum_first) for r in (8, 2)],
            input_output_aliases=aliases,
            scratch_shapes=[
                pltpu.VMEM((2, WIN, 2 * ROWS), f32),
                pltpu.VMEM((lanes, HD), bf16),
                pltpu.VMEM((lanes, HD), bf16),
                pltpu.VMEM((HD, lanes), bf16),
                pltpu.VMEM((WIN, HD), bf16),
                pltpu.VMEM((WIN, HD), bf16),
                pltpu.VMEM((HD, WIN), bf16),
                pltpu.VMEM((WIN, HD), f32),
                pltpu.VMEM((WIN, HD), f32),
            ],
            compiler_params=params(60),
            cost_estimate=cost(count * lanes * WIN * HD * 2 * 10, 8 << 20, count * lanes * WIN),
            name="attend",
        )(*operands)
        rows, sums[part] = result[:6], result[6:]
        if first + count == sum_first + sum_count:
            terms, far = sums[part]
            rings = [[4 * z + i for i in range(4)] for z in range(seq_count // 4)]
            terms = lax.all_to_all(
                terms, "seq", split_axis=0, concat_axis=0, axis_index_groups=rings, tiled=True
            )
            partial[part] = [terms, far]

    rests = []
    for part, (_, count) in enumerate(SUMS):
        terms, far = partial[part]
        terms, _ = lax.optimization_barrier((terms, partial[len(SUMS) - 1][1]))
        rest = pl.pallas_call(
            pass_on,
            out_shape=shape(2 * ROWS, count * 2 * HD),
            in_specs=[SMEM] + [pl.BlockSpec(memory_space=pltpu.VMEM)] * 2,
            compiler_params=params(32),
            cost_estimate=cost(1e6, 2 << 20),
            name="pass_on",
        )(x, terms, far)
        rests.append(earlier(rest, BACK))
        partial[part] = [terms, rests[part]]
    gradients = [rows[0]]
    for k, piece in zip((1,) + NEAR, rows[1:]):
        if k in (3, 7):
            piece, _ = lax.optimization_barrier((piece, rests[0]))
        gradients.append(swap(piece, k))

    spread, _ = lax.optimization_barrier((spread, gradients[1:]))
    message = pl.pallas_call(
        return_keys,
        out_shape=shape(GROUPS * MSG, wide),
        compiler_params=params(32),
        in_specs=[SMEM] + [pl.BlockSpec(memory_space=pltpu.VMEM)] * (1 + 2 * len(SUMS)),
        cost_estimate=cost(1e8, 3 << 20),
        name="return_keys",
    )(x, spread, *partial[0], *partial[1])
    message = lax.all_to_all(message, "grp", split_axis=0, concat_axis=0, tiled=True)

    grad_query = pl.pallas_call(
        unpack_rows,
        grid=(KVH,),
        out_shape=shape(ROWS, KVH * WIDE),
        in_specs=[full(ROWS, PAIR)] + [columns(2 * CAP, WIDE)] * 2 + [columns(2 * CAP, WIDE // 2)] * 4,
        out_specs=columns(ROWS, WIDE),
        compiler_params=params(60),
        cost_estimate=cost(4e8, 6 << 20),
        name="unpack_rows",
    )(order, *gradients)

    grad_key, grad_value = pl.pallas_call(
        unpack_keys,
        out_shape=[shape(ROWS, KVH * HD)] * 2,
        compiler_params=params(32),
        cost_estimate=cost(1e8, 1 << 20),
        name="unpack_keys",
    )(sort, message)
    return (grad_query, grad_key, grad_value)


def solution(mesh):
    in_specs = (
        P(("grp", "seq"), None),
        P(("grp", "seq"), None),
        P(("grp", "seq"), None),
        P(("grp", "seq"), None),
        P(("grp", "seq")),
        P("grp", None),
    )
    out_specs = (P(("grp", "seq"), None), P(("grp", "seq"), None), P(("grp", "seq"), None))
    return jax.shard_map(
        on_device, mesh=mesh, in_specs=in_specs, out_specs=out_specs, check_vma=False
    )
```

```python
import functools

import jax
import jax.numpy as jnp
from jax import lax
from jax.experimental import pallas as pl
from jax.experimental.pallas import tpu as pltpu
from jax.sharding import PartitionSpec as P

HD = 128
KVH = 4
GQ = 16
DOCS = 16
ROWS = 128
CAP = 24
BACK = 4
WIN = (BACK + 1) * ROWS
EARLY = 2
CALLS = ((0, EARLY, 0), (EARLY, KVH - EARLY, 1))
SUMS = ((0, EARLY), (EARLY, KVH - EARLY))
WIDE = GQ * HD
SCALE = HD**-0.5
LOG2E = 1.4426950408889634
GROUPS = 8
FAR = 4
NEAR = (2, 3, 6, 7)
MSG = 2 * CAP
BSLOT = 64
PAIR = 256
A_PAIRS = GQ * ROWS // PAIR
B_PAIRS = GQ * BSLOT // PAIR
UNROLL = 4
f32, bf16, i32 = jnp.float32, jnp.bfloat16, jnp.int32
NT = (((1,), (1,)), ((), ()))


def dot(a, b, dims=None):
    if dims is None:
        return jnp.dot(a, b, preferred_element_type=f32)
    return lax.dot_general(a, b, dims, preferred_element_type=f32)


def iota(shape, dim):
    return lax.broadcasted_iota(i32, shape, dim)


def params(mib):
    return pltpu.CompilerParams(vmem_limit_bytes=mib * 1024 * 1024)


def arrival(group, hot, before, axis):
    if axis == 0:
        earlier = dot(hot.astype(bf16), before.astype(bf16))
    else:
        earlier = dot(before.astype(bf16), hot.astype(bf16))
    return jnp.sum(hot * earlier, axis=axis, keepdims=True).astype(i32)


def pack_keys(me_ref, length_ref, row_ref, col_ref, key_ref, value_ref, out_ref, order_ref, sort_ref):
    me = me_ref[0]
    group = row_ref[...] >> 12
    hot = (iota((GROUPS, ROWS), 0) == group).astype(f32)
    rank = arrival(group, hot, iota((ROWS, ROWS), 0) < iota((ROWS, ROWS), 1), 0)
    n = iota((GROUPS * MSG, ROWS), 0)
    both = (n == group * MSG + rank) | (n == (group ^ FAR) * MSG + CAP + rank)
    target = col_ref[...]
    group = target >> 12
    hot = (iota((ROWS, ROWS), 1) == group).astype(f32)
    rank = arrival(group, hot, iota((ROWS, ROWS), 1) < iota((ROWS, ROWS), 0), 1)
    order_ref[...] = (iota((ROWS, PAIR), 1) == (group ^ me) * CAP + rank).astype(bf16)
    n = iota((ROWS, GROUPS * MSG), 1)
    sort_ref[...] = ((n == group * MSG + rank) | (n == (group ^ FAR) * MSG + CAP + rank)).astype(bf16)
    lane = iota((1, HD), 1)
    slot = jnp.where(iota((ROWS, HD), 1) == 0, (target & (ROWS - 1)) + 1, 0).astype(f32).astype(bf16)
    extra = jnp.zeros((1, HD), i32)
    for k in range(DOCS):
        extra = jnp.where(lane == DOCS + k, length_ref[k] >> 8, extra)
        extra = jnp.where(lane == 2 * DOCS + k, length_ref[k] & 255, extra)
    parts = []
    for j in range(KVH):
        parts += [key_ref[:, j * HD : (j + 1) * HD], value_ref[:, j * HD : (j + 1) * HD]]
    packed = dot(both.astype(bf16), jnp.concatenate(parts + [slot], axis=1))
    out_ref[:, : KVH * 2 * HD] = packed[:, : KVH * 2 * HD].astype(bf16)
    out_ref[:, KVH * 2 * HD :] = (packed[:, KVH * 2 * HD :] + extra.astype(f32)).astype(bf16)


def pack_rows(blocks, me_ref, target_ref, mate_target_ref, query_ref, grad_ref, mate_query_ref, mate_grad_ref, _, *refs):
    outs, picks_ref = refs[:-1], refs[-1]
    @pl.when(pl.program_id(0) == 0)
    def _():
        for loader, ref in enumerate((target_ref, mate_target_ref)):
            group = ref[...] >> 12
            hot = (iota((GROUPS, ROWS), 0) == group).astype(f32)
            rank = arrival(group, hot, iota((ROWS, ROWS), 0) < iota((ROWS, ROWS), 1), 0)
            offset = group ^ me_ref[0]
            place = jnp.where((offset & 1) == 0, (offset >> 1) * MSG + loader * CAP + rank, -1)
            picks_ref[loader] = (iota((GROUPS * CAP, ROWS), 0) == place).astype(bf16)

    picks = [
        jnp.concatenate([picks_ref[loader, i * MSG : (i + 1) * MSG, :] for i in blocks], axis=0)
        for loader in range(2)
    ]
    query = dot(picks[0], query_ref[...]) + dot(picks[1], mate_query_ref[...])
    grad = dot(picks[0], grad_ref[...]) + dot(picks[1], mate_grad_ref[...])
    for i, ref in enumerate(outs):
        at = slice(i * MSG, (i + 1) * MSG)
        ref[...] = jnp.concatenate([query[at], grad[at]], axis=0).astype(bf16)


def starts_of(lengths, position):
    before = (iota((HD, HD), 0) <= iota((HD, HD), 1)).astype(bf16)
    high, low = lengths
    ends = 256.0 * dot(high.astype(bf16), before) + dot(low.astype(bf16), before)
    ends = jnp.broadcast_to(ends[0:1], (ROWS, HD))
    held = (ends <= position.astype(f32)) & (iota((ROWS, HD), 1) < DOCS)
    return jnp.max(jnp.where(held, ends, 0.0), axis=1, keepdims=True)


def group_keys(me_ref, seq_ref, msg_ref, whole_ref, early_ref, late_ref, spread_ref, dense_ref, back_ref, vec_ref):
    wide = KVH * 2 * HD
    me = me_ref[0]
    first = (seq_ref[0] - BACK) * ROWS
    slot = msg_ref[:, wide : wide + 1].astype(f32)
    n, r = iota((GROUPS * MSG, ROWS), 0), iota((GROUPS * MSG, ROWS), 1)
    side_of = jnp.zeros_like(n)
    for k in range(GROUPS):
        side_of = jnp.where((n >= k * MSG + CAP) & (n < (k + 1) * MSG), 1, side_of)
    whole = []
    for side in range(2):
        hot = ((slot == (r + 1).astype(f32)) & (side_of == side)).astype(f32)
        spread_ref[side * GROUPS * MSG : (side + 1) * GROUPS * MSG, :] = hot.astype(bf16)
        whole.append(dot(jnp.transpose(hot).astype(bf16), msg_ref[:, :wide]).astype(bf16))
    whole_ref[...] = jnp.concatenate(whole, axis=0)
    for ref, at in ((early_ref, slice(0, EARLY * 2 * HD)), (late_ref, slice(EARLY * 2 * HD, wide))):
        ref[...] = jnp.concatenate([w[:, at] for w in whole], axis=0)

    def message(k):
        at = pl.multiple_of((me ^ k) * MSG, MSG)
        return msg_ref[pl.ds(at, MSG), wide : wide + HD].astype(f32)

    from_own, from_core = message(0), message(1)
    a_slots = [m[:CAP, :1] for m in [from_own, from_core] + [message(k) for k in NEAR]]
    twice = []
    for i in range(0, 6, 2):
        twice += a_slots[i : i + 2] * 2
    rows = 12 * CAP
    column = jnp.concatenate(twice + [jnp.zeros((384 - rows, 1), f32)], axis=0)
    lane = iota((384, 2 * ROWS), 1)
    n = iota((384, 2 * ROWS), 0)
    is_grad = jnp.zeros_like(n)
    for k in range(3):
        is_grad = jnp.where((n >= (2 * k + 1) * MSG) & (n < (2 * k + 2) * MSG), 1, is_grad)
    hot = (column == ((lane & (ROWS - 1)) + 1).astype(f32)) & (is_grad == (lane >> 7))
    dense_ref[...] = jnp.transpose(hot.astype(f32)).astype(bf16)
    column = jnp.concatenate(a_slots, axis=0)
    back_ref[...] = (column == (iota((6 * CAP, ROWS), 1) + 1).astype(f32)).astype(bf16)

    def lengths(rows):
        rows = jnp.broadcast_to(rows[:1], (8, HD))
        pick = (iota((HD, HD), 0) == iota((HD, HD), 1) + DOCS).astype(bf16)
        high = dot(rows.astype(bf16), pick)
        pick = (iota((HD, HD), 0) == iota((HD, HD), 1) + 2 * DOCS).astype(bf16)
        return high, dot(rows.astype(bf16), pick)

    row, column = iota((ROWS, ROWS), 0), iota((ROWS, ROWS), 1)
    position = iota((ROWS, 1), 0) + first + BACK * ROWS
    gap = jnp.zeros((BSLOT - 2 * CAP, 1), f32)
    half = [from_own[CAP:, :1], from_core[CAP:, :1], gap]
    arrived = jnp.concatenate(half + half, axis=0)
    hot_b = jnp.transpose((arrived == (column + 1).astype(f32)).astype(f32))
    hots = ((row == column).astype(f32), hot_b)
    for side in range(2):
        start = starts_of(lengths(from_own if side == 0 else message(FAR)), position) - first.astype(f32)
        low = jnp.sum(hots[side] * start, axis=0, keepdims=True)
        high = jnp.sum(hots[side] * (row + BACK * ROWS).astype(f32), axis=0, keepdims=True)
        vec_ref[2 * side : 2 * side + 1, :] = low.astype(i32)
        vec_ref[2 * side + 1 : 2 * side + 2, :] = high.astype(i32)
    vec_ref[4:8, :] = jnp.zeros((4, ROWS), i32)


def attend(x_ref, dense_ref, back_ref, vec_ref, *refs):
    ins, refs = refs[:4], refs[4:]
    window, refs = refs[: BACK + 1], refs[BACK + 1 :]
    refs = refs[len(refs) - 9 - 8 :]
    outs, refs = refs[:6], refs[6:]
    (sums_ref, far_ref), refs = refs[:2], refs[2:]
    bias_ref, q_ref, g_ref, dq_ref, key_ref, value_ref, flip_ref, dk_ref, dv_ref = refs

    @pl.when(pl.program_id(0) == 0)
    def _():
        c = iota((WIN, ROWS), 0)
        for side in range(2):
            low, high = vec_ref[2 * side : 2 * side + 1, :], vec_ref[2 * side + 1 : 2 * side + 2, :]
            bias = jnp.where((c >= low) & (c <= high), 0.0, -1e30).astype(f32)
            bias_ref[side, :, 0:ROWS] = bias
            bias_ref[side, :, ROWS : 2 * ROWS] = bias

    pieces = [r[...] for r in ins[:3]]
    pieces.append(jnp.zeros((384 - 12 * CAP, WIDE), bf16))
    rows_a = dot(dense_ref[...], jnp.concatenate(pieces, axis=0)).astype(bf16)
    gap = jnp.zeros((BSLOT - MSG, WIDE), bf16)
    rows_b = jnp.concatenate([ins[3][:MSG], gap, ins[3][MSG:], gap], axis=0)
    for h in range(GQ):
        at = slice(h * HD, (h + 1) * HD)
        q_ref[h * ROWS : (h + 1) * ROWS, :] = rows_a[:ROWS, at]
        g_ref[h * ROWS : (h + 1) * ROWS, :] = rows_a[ROWS:, at]
        to = GQ * ROWS + h * BSLOT
        q_ref[to : to + BSLOT, :] = rows_b[:BSLOT, at]
        g_ref[to : to + BSLOT, :] = rows_b[BSLOT:, at]

    for side in range(2):
        for k in range(BACK + 1):
            part = window[k][side * ROWS : (side + 1) * ROWS, :]
            key_ref[k * ROWS : (k + 1) * ROWS, :] = part[:, :HD]
            value_ref[k * ROWS : (k + 1) * ROWS, :] = part[:, HD:]
            flip_ref[:, k * ROWS : (k + 1) * ROWS] = jnp.transpose(part[:, :HD].astype(f32)).astype(bf16)
        dk_ref[...] = jnp.zeros_like(dk_ref)
        dv_ref[...] = jnp.zeros_like(dv_ref)

        def pair(at):
            q, g = q_ref[pl.ds(at, PAIR), :], g_ref[pl.ds(at, PAIR), :]
            scores = dot(key_ref[...], q, NT) * (SCALE * LOG2E) + bias_ref[side]
            powers = jnp.exp2(scores - jnp.max(scores, axis=0, keepdims=True))
            probs = powers * (1.0 / jnp.sum(powers, axis=0, keepdims=True))
            dprobs = dot(value_ref[...], g, NT)
            weighted = probs * dprobs
            delta = jnp.sum(weighted, axis=0, keepdims=True)
            return probs.astype(bf16), (weighted - probs * delta).astype(bf16)

        @pl.loop(0, (B_PAIRS if side else A_PAIRS) // UNROLL)
        def _(step):
            wide = UNROLL * PAIR
            at = pl.multiple_of(step * wide + (A_PAIRS * PAIR if side else 0), PAIR)
            parts = [pair(at + u * PAIR) for u in range(UNROLL)]
            probs = jnp.concatenate([p for p, _ in parts], axis=1)
            dscores = jnp.concatenate([d for _, d in parts], axis=1)
            dv_ref[...] += dot(probs, g_ref[pl.ds(at, wide), :])
            dk_ref[...] += dot(dscores, q_ref[pl.ds(at, wide), :])
            dq_ref[:, pl.ds(at, wide)] = (dot(flip_ref[...], dscores) * SCALE).astype(bf16)

        for k in range(BACK + 1):
            at = slice(k * ROWS, (k + 1) * ROWS)
            both = jnp.concatenate([dk_ref[at, :] * SCALE, dv_ref[at, :]], axis=1).astype(bf16)
            if k == 0:
                far_ref[side * ROWS : (side + 1) * ROWS, :] = both
            else:
                to = ((x_ref[0] + k) & 3) * (2 * ROWS) + side * ROWS
                sums_ref[pl.ds(pl.multiple_of(to, ROWS), ROWS), :] = both

    back = back_ref[...]
    eye = (iota((ROWS, ROWS), 0) == iota((ROWS, ROWS), 1)).astype(bf16)
    straight = []
    for i in range(GQ // 2):
        from_ = GQ * ROWS + i * ROWS
        straight.append(dot(eye, dq_ref[:, from_ : from_ + ROWS], NT))
    for h in range(GQ):
        at = slice(h * HD, (h + 1) * HD)
        rows = dot(back, dq_ref[:, h * ROWS : (h + 1) * ROWS], NT)
        low = h % 2 * BSLOT
        extra = straight[h // 2][low : low + 2 * CAP]
        outs[0][:, at] = jnp.concatenate([rows[:CAP], extra[:CAP]], axis=0).astype(bf16)
        outs[1][:, at] = jnp.concatenate([rows[CAP : 2 * CAP], extra[CAP:]], axis=0).astype(bf16)
        if h < GQ // 2:
            early = rows if h == 0 else jnp.concatenate([early, rows], axis=1)
        else:
            late = rows if h == GQ // 2 else jnp.concatenate([late, rows], axis=1)
    for k in range(4):
        at = slice((k + 2) * CAP, (k + 3) * CAP)
        outs[k + 2][...] = jnp.concatenate([early[at], late[at]], axis=0).astype(bf16)


def add_blocks(x_ref, ref, later):
    total = jnp.zeros((2 * ROWS, ref.shape[1]), f32)
    for j in range(4):
        weight = jnp.where((j >= x_ref[0]) == later, 1.0, 0.0).astype(f32)
        total = total + ref[j * 2 * ROWS : (j + 1) * 2 * ROWS, :].astype(f32) * weight
    return total


def pass_on(x_ref, sums_ref, far_ref, out_ref):
    out_ref[...] = (add_blocks(x_ref, sums_ref, False) + far_ref[...].astype(f32)).astype(bf16)


def return_keys(x_ref, spread_ref, *refs):
    ins, out_ref = refs[:-1], refs[-1]
    size = GROUPS * MSG
    for part, (first, count) in enumerate(SUMS):
        total = add_blocks(x_ref, ins[2 * part], True) + ins[2 * part + 1][...].astype(f32)
        total = total.astype(bf16)
        rows = dot(spread_ref[:size, :], total[:ROWS]) + dot(spread_ref[size:, :], total[ROWS:])
        out_ref[:, first * 2 * HD : (first + count) * 2 * HD] = rows.astype(bf16)


def unpack_keys(sort_ref, msg_ref, key_ref, value_ref):
    rows = dot(sort_ref[...], msg_ref[...]).astype(bf16)
    for j in range(KVH):
        key_ref[:, j * HD : (j + 1) * HD] = rows[:, 2 * j * HD : (2 * j + 1) * HD]
        value_ref[:, j * HD : (j + 1) * HD] = rows[:, (2 * j + 1) * HD : (2 * j + 2) * HD]


def unpack_rows(order_ref, own_ref, core_ref, *refs):
    near, out_ref = refs[:4], refs[-1]
    own, core = own_ref[...].astype(f32), core_ref[...].astype(f32)
    near = [r[...].astype(f32) for r in near]
    near = [jnp.concatenate([r[:CAP], r[CAP:]], axis=1) for r in near]
    rows = [own[:CAP], core[:CAP], near[0], near[1], own[CAP:], core[CAP:], near[2], near[3]]
    rows.append(jnp.zeros((PAIR - 8 * CAP, WIDE), f32))
    out_ref[...] = dot(order_ref[...], jnp.concatenate(rows, axis=0).astype(bf16)).astype(bf16)


def shape(*dims, dtype=bf16):
    return jax.ShapeDtypeStruct(dims, dtype)


def full(*dims):
    return pl.BlockSpec(dims, lambda *_: (0,) * len(dims))


def columns(rows, wide, first=0):
    return pl.BlockSpec((rows, wide), lambda i: (0, first + i))


SMEM = pl.BlockSpec(memory_space=pltpu.SMEM)


def cost(flops, size, powers=0):
    return pl.CostEstimate(flops=int(flops), bytes_accessed=int(size), transcendentals=int(powers))


def on_device(queries, key_rows, value_rows, grad_rows, targets, doc_lengths):
    seq_count = lax.axis_size("seq")
    me = lax.axis_index("grp").astype(i32).reshape(1)
    seq = lax.axis_index("seq").astype(i32).reshape(1)

    def swap(tensor, k):
        return lax.ppermute(tensor, "grp", [(i, i ^ k) for i in range(GROUPS)])

    def later(tensor, distance):
        return lax.ppermute(tensor, "seq", [(i, (i + distance) % seq_count) for i in range(seq_count)])

    def earlier(tensor, distance):
        return lax.ppermute(tensor, "seq", [((i + distance) % seq_count, i) for i in range(seq_count)])

    wide = KVH * 2 * HD
    message, order, sort = pl.pallas_call(
        pack_keys,
        out_shape=[
            shape(GROUPS * MSG, wide + HD),
            shape(ROWS, PAIR),
            shape(ROWS, GROUPS * MSG),
        ],
        in_specs=[SMEM] * 2 + [pl.BlockSpec(memory_space=pltpu.VMEM)] * 4,
        compiler_params=params(32),
        cost_estimate=cost(1e8, 1 << 20),
        name="pack_keys",
    )(me, doc_lengths[0], targets.reshape(1, ROWS), targets.reshape(ROWS, 1), key_rows, value_rows)
    message = lax.all_to_all(message, "grp", split_axis=0, concat_axis=0, tiled=True)

    step = 1024
    mate_target = swap(targets, 1)
    mate_query, mate_grad = swap(queries, 1), swap(grad_rows, 1)
    def pack(blocks, first, count, after):
        return pl.pallas_call(
            functools.partial(pack_rows, blocks),
            grid=(count * WIDE // step,),
            out_shape=[shape(2 * MSG, count * WIDE)] * len(blocks),
            in_specs=[SMEM]
            + [full(1, ROWS)] * 2
            + [columns(ROWS, step, first * (WIDE // step))] * 4
            + [pl.BlockSpec(memory_space=pl.ANY)],
            out_specs=[columns(2 * MSG, step)] * len(blocks),
            scratch_shapes=[pltpu.VMEM((2, GROUPS * CAP, ROWS), bf16)],
            compiler_params=params(60),
            cost_estimate=cost(count * 1e8, count * 2 << 20),
            name="pack_rows",
        )(me, targets.reshape(1, ROWS), mate_target.reshape(1, ROWS), queries, grad_rows, mate_query, mate_grad, after)

    early = pack((1, 3), 0, EARLY, order)
    late = pack((1, 3), EARLY, KVH - EARLY, order)
    *rows, message = lax.optimization_barrier((*early, *late, message))
    early, late = rows[:2], rows[2:]
    early = [swap(early[0], 2), swap(early[1], 6)]

    whole, *own, spread, dense, back, vec = pl.pallas_call(
        group_keys,
        out_shape=[
            shape(2 * ROWS, wide),
            shape(2 * ROWS, EARLY * 2 * HD),
            shape(2 * ROWS, wide - EARLY * 2 * HD),
            shape(2 * GROUPS * MSG, ROWS),
            shape(2 * ROWS, 384),
            shape(6 * CAP, ROWS),
            shape(8, ROWS, dtype=i32),
        ],
        in_specs=[SMEM] * 2 + [pl.BlockSpec(memory_space=pltpu.VMEM)],
        compiler_params=params(32),
        cost_estimate=cost(2e8, 2 << 20),
        name="group_keys",
    )(me, seq, message)

    x = seq & 3
    whole = later(whole, 3)
    staying = [pack((0, 2), first, count, order) for first, count, _ in CALLS]
    windows = []
    for stage, part in enumerate(own):
        window = {d: later(part, d) for d in (4, 2)}
        held = part
        if stage == 0:
            held, *rest = lax.optimization_barrier((part, *staying[0], *staying[1]))
            staying = [rest[:2], rest[2:]]
        window[1] = later(held, 1)
        window[0] = part
        window[3] = whole
        windows.append([window[d] for d in range(BACK, -1, -1)])
        if stage == 0:
            late = lax.optimization_barrier((*late, *early, part))[:2]
            late = [swap(late[0], 2), swap(late[1], 6)]
    lanes = GQ * (ROWS + BSLOT)
    rows, sums, partial = None, {}, {}
    for first, count, part in CALLS:
        stage, row_at, (sum_first, sum_count) = part, 0, SUMS[part]
        here = staying[part]
        operands = [x, dense, back, vec, here[0], *(late if stage else early), here[1], *windows[stage]]
        fixed = len(operands)
        aliases, outputs = {}, 0
        for begun, size in ((rows, 6), (sums.get(part), 2)):
            for i, array in enumerate(begun or ()):
                aliases[len(operands)] = outputs + i
                operands.append(array)
            outputs += size
        result = pl.pallas_call(
            attend,
            grid=(count,),
            out_shape=[shape(2 * CAP, KVH * WIDE)] * 2
            + [shape(2 * CAP, KVH * WIDE // 2)] * 4
            + [shape(8 * ROWS, sum_count * 2 * HD), shape(2 * ROWS, sum_count * 2 * HD)],
            in_specs=[SMEM, full(2 * ROWS, 384), full(6 * CAP, ROWS), full(8, ROWS)]
            + [columns(2 * MSG, WIDE, at) for at in (row_at,) * 4]
            + [columns(2 * ROWS, 2 * HD, first if d == 3 else row_at) for d in range(BACK, -1, -1)]
            + [pl.BlockSpec(memory_space=pl.ANY)] * (len(operands) - fixed),
            out_specs=[columns(2 * CAP, WIDE, first)] * 2
            + [columns(2 * CAP, WIDE // 2, first)] * 4
            + [columns(r * ROWS, 2 * HD, first - sum_first) for r in (8, 2)],
            input_output_aliases=aliases,
            scratch_shapes=[
                pltpu.VMEM((2, WIN, 2 * ROWS), f32),
                pltpu.VMEM((lanes, HD), bf16),
                pltpu.VMEM((lanes, HD), bf16),
                pltpu.VMEM((HD, lanes), bf16),
                pltpu.VMEM((WIN, HD), bf16),
                pltpu.VMEM((WIN, HD), bf16),
                pltpu.VMEM((HD, WIN), bf16),
                pltpu.VMEM((WIN, HD), f32),
                pltpu.VMEM((WIN, HD), f32),
            ],
            compiler_params=params(60),
            cost_estimate=cost(count * lanes * WIN * HD * 2 * 10, 8 << 20, count * lanes * WIN),
            name="attend",
        )(*operands)
        rows, sums[part] = result[:6], result[6:]
        if first + count == sum_first + sum_count:
            terms, far = sums[part]
            rings = [[4 * z + i for i in range(4)] for z in range(seq_count // 4)]
            terms = lax.all_to_all(
                terms, "seq", split_axis=0, concat_axis=0, axis_index_groups=rings, tiled=True
            )
            partial[part] = [terms, far]

    rests = []
    for part, (_, count) in enumerate(SUMS):
        terms, far = partial[part]
        terms, _ = lax.optimization_barrier((terms, partial[len(SUMS) - 1][1]))
        rest = pl.pallas_call(
            pass_on,
            out_shape=shape(2 * ROWS, count * 2 * HD),
            in_specs=[SMEM] + [pl.BlockSpec(memory_space=pltpu.VMEM)] * 2,
            compiler_params=params(32),
            cost_estimate=cost(1e6, 2 << 20),
            name="pass_on",
        )(x, terms, far)
        rests.append(earlier(rest, BACK))
        partial[part] = [terms, rests[part]]
    gradients = [rows[0]]
    for k, piece in zip((1,) + NEAR, rows[1:]):
        if k in (3, 7):
            piece, _ = lax.optimization_barrier((piece, rests[0]))
        gradients.append(swap(piece, k))

    spread, _ = lax.optimization_barrier((spread, gradients[1:]))
    message = pl.pallas_call(
        return_keys,
        out_shape=shape(GROUPS * MSG, wide),
        compiler_params=params(32),
        in_specs=[SMEM] + [pl.BlockSpec(memory_space=pltpu.VMEM)] * (1 + 2 * len(SUMS)),
        cost_estimate=cost(1e8, 3 << 20),
        name="return_keys",
    )(x, spread, *partial[0], *partial[1])
    message = lax.all_to_all(message, "grp", split_axis=0, concat_axis=0, tiled=True)

    grad_query = pl.pallas_call(
        unpack_rows,
        grid=(KVH,),
        out_shape=shape(ROWS, KVH * WIDE),
        in_specs=[full(ROWS, PAIR)] + [columns(2 * CAP, WIDE)] * 2 + [columns(2 * CAP, WIDE // 2)] * 4,
        out_specs=columns(ROWS, WIDE),
        compiler_params=params(60),
        cost_estimate=cost(4e8, 6 << 20),
        name="unpack_rows",
    )(order, *gradients)

    grad_key, grad_value = pl.pallas_call(
        unpack_keys,
        out_shape=[shape(ROWS, KVH * HD)] * 2,
        compiler_params=params(32),
        cost_estimate=cost(1e8, 1 << 20),
        name="unpack_keys",
    )(sort, message)
    return (grad_query, grad_key, grad_value)


def solution(mesh):
    in_specs = (
        P(("grp", "seq"), None),
        P(("grp", "seq"), None),
        P(("grp", "seq"), None),
        P(("grp", "seq"), None),
        P(("grp", "seq")),
        P("grp", None),
    )
    out_specs = (P(("grp", "seq"), None), P(("grp", "seq"), None), P(("grp", "seq"), None))
    return jax.shard_map(
        on_device, mesh=mesh, in_specs=in_specs, out_specs=out_specs, check_vma=False
    )
```
